512 devices in a mesh: dp: 16 (over y, x_lo, core), ctx: 32 (over z, x_hi).
Axes of the slice: x: 4 (x_hi: 2, x_lo: 2; x = x_hi * 2 + x_lo), y: 4, z: 16, core: 2. Of those that a mesh axis runs over, the one named last changes fastest.
Arguments:
- queries: bfloat16 [16, 4096, 2048], P('dp', 'ctx'), may hold values from -8 to 8
- keys: bfloat16 [16, 4096, 2048], P('dp', 'ctx'), may hold values from -8 to 8
- values: bfloat16 [16, 4096, 2048], P('dp', 'ctx'), may hold values from -4.1875 to 4.1875
- out_grad: bfloat16 [16, 4096, 2048], P('dp', 'ctx'), may hold values from -15 to 15
- log_norm: bfloat16 [16, 4096, 16], P('dp', 'ctx'), may hold values from 6.78125 to 8.1875
- row_delta: bfloat16 [16, 4096, 16], P('dp', 'ctx'), may hold values from -48 to 48
- doc_lengths: int32 [16, 8, 4], replicated, may hold values from 0 to 4, as said below
- bin_dest: int32 [16, 8], replicated, may hold values from 0 to 15, as said below
Outputs:
- query_grad: bfloat16 [16, 4096, 2048], P('dp', 'ctx')
- key_grad: bfloat16 [16, 4096, 2048], P('dp', 'ctx')
- value_grad: bfloat16 [16, 4096, 2048], P('dp', 'ctx')
The draws below stay inside these ranges and needn't reach their ends.
Inputs may be any that keep to these rules, and one draw needn't show every extreme that they name: doc_lengths[g, b] lists the lengths in blocks of the documents that fill bin b of row g, in order, followed by zeros; they sum to 4; some bin is a single document. bin_dest[g, b] is g or g XOR (8); where it is the other group, that group's bin b has destination g.
All inputs are finite; a program needn't handle non-finite values.
Results may differ from the reference program's by a relative error of at most 0.0085.
Values may be sent and summed in bfloat16 or wider, within the bound.
No kernel may reach another device: no remote copies, remote signals or barrier semaphores. Data moves between devices by JAX's collectives and lax.ppermute only.
A program may use at most 64 MiB of HBM per device.

```python
import math
import jax
import jax.numpy as jnp
from jax import lax

H = 16
HD = 128
BLOCK = 128
TOK_DEV = 128
FEAT = 2048
ROW = 4096
ROWS = 16
BINS = 8
BIN_BLOCKS = 4


def draw_doc_lengths(key, part):
    key = jax.random.fold_in(key, 11)
    cut_key, pick_key = jax.random.split(key)
    cuts = jax.random.randint(cut_key, (ROWS, BINS, BIN_BLOCKS), 0, 2)
    chosen = jax.random.randint(pick_key, (), 0, ROWS * BINS)
    flat_index = jnp.arange(ROWS * BINS).reshape(ROWS, BINS)
    cuts = jnp.where((flat_index == chosen)[:, :, None], 0, cuts)
    first_block = (jnp.arange(BIN_BLOCKS) == 0).astype(jnp.int32)
    starts = jnp.maximum(cuts, first_block[None, None, :])
    doc_number = jnp.cumsum(starts, axis=2) - 1
    slots = jnp.arange(BIN_BLOCKS)[None, None, None, :]
    lengths = jnp.sum((doc_number[:, :, :, None] == slots).astype(jnp.int32), axis=2)
    return lengths.astype(jnp.int32)


def draw_bin_dest(key, part):
    key = jax.random.fold_in(key, 23)
    half_rows = ROWS // 2
    flips = jax.random.randint(key, (half_rows, BINS), 0, 2)
    both_halves = jnp.concatenate([flips, flips], axis=0)
    row_index = jnp.arange(ROWS)[:, None]
    partner = jnp.bitwise_xor(row_index, half_rows)
    return jnp.where(both_halves == 1, partner, row_index).astype(jnp.int32)


def shard_levels(rng, shape, cuts, smallest, high):
    def one(axis_at, parts):
        heights = jax.random.uniform(jax.random.fold_in(jax.random.fold_in(rng, 6), axis_at), (parts,), jnp.float32, smallest / len(cuts), high / len(cuts))
        return jnp.repeat(jnp.exp(heights), shape[axis_at] // parts).reshape((-1,) + (1,) * (len(shape) - axis_at - 1))

    loudness = one(*cuts[0])
    for cut in cuts[1:]:
        loudness = loudness * one(*cut)
    return loudness


def normal_values(rng, extent, scale, reach, cuts=(), held_as=jnp.bfloat16):
    result = jax.random.normal(rng, extent, jnp.float32) * scale
    if len(cuts) > 0:
        result = shard_levels(rng, extent, cuts, -0.22, 0.18) * result
    return jnp.clip(result, min=-reach, max=reach).astype(held_as)


def setup_inputs(seed: int = 0) -> dict:
    seeds = jax.random.split(jax.random.key(seed), 9)
    queries = normal_values(seeds[0], (ROWS, ROW, FEAT), 1.4, 8.0, ((0, 16), (1, 32)))
    keys = normal_values(seeds[1], (ROWS, ROW, FEAT), 1.4, 8.0, ((0, 16), (1, 32)))
    values = normal_values(seeds[2], (ROWS, ROW, FEAT), 0.7, 4.1875, ((0, 16), (1, 32)))
    out_grad = normal_values(seeds[3], (ROWS, ROW, FEAT), 2.5, 15.0, ((0, 16), (1, 32)))
    log_norm = jnp.clip(6.78125 + 1.40625 * jax.random.uniform(seeds[4], (ROWS, ROW, H), jnp.float32) ** shard_levels(seeds[4], (ROWS, ROW, H), ((0, 16), (1, 32)), -0.2, 0.2), 6.78125, 8.1875).astype(jnp.bfloat16)
    row_delta = normal_values(seeds[5], (ROWS, ROW, H), 8.0, 48.0, ((0, 16), (1, 32)))
    doc_lengths = draw_doc_lengths(jax.random.fold_in(seeds[8], 71), 0)
    bin_dest = draw_bin_dest(jax.random.fold_in(seeds[8], 71), 0)
    return {"queries": queries, "keys": keys, "values": values, "out_grad": out_grad, "log_norm": log_norm, "row_delta": row_delta, "doc_lengths": doc_lengths, "bin_dest": bin_dest}


def bin_docs(lengths_row, token_count):
    doc_ends = jnp.cumsum(lengths_row).astype(jnp.int32)
    block_index = jnp.arange(token_count, dtype=jnp.int32) // BLOCK
    return lax.optimization_barrier(jnp.sum((doc_ends[None, :] <= block_index[:, None]).astype(jnp.int32), axis=1))

def bin_backward(packed):
    queries, keys, values, out_grad, log_norm, row_delta, lengths_row = packed
    span = queries.shape[0]
    inv_root = 1.0 / math.sqrt(HD)
    query_heads = queries.astype(jnp.float32).reshape(span, H, HD)
    key_heads = keys.astype(jnp.float32).reshape(span, H, HD)
    value_heads = values.astype(jnp.float32).reshape(span, H, HD)
    grad_heads = out_grad.astype(jnp.float32).reshape(span, H, HD)
    scores = jnp.einsum('qhd,khd->hqk', query_heads, key_heads, precision=lax.Precision.HIGHEST) * inv_root
    doc_index = bin_docs(lengths_row, span)
    same_doc = (doc_index[:, None] == doc_index[None, :])[None]
    norm_column = jnp.transpose(log_norm.astype(jnp.float32))[:, :, None]
    delta_column = jnp.transpose(row_delta.astype(jnp.float32))[:, :, None]
    probs = jnp.where(same_doc, jnp.exp(scores - norm_column), 0.0)
    probs_low = probs.astype(jnp.bfloat16)
    dprobs = jnp.einsum('qhd,khd->hqk', grad_heads, value_heads, precision=lax.Precision.HIGHEST)
    dscores = probs * (dprobs - delta_column)
    dscores_low = dscores.astype(jnp.bfloat16)
    dscores_wide = dscores_low.astype(jnp.float32)
    query_grad = (jnp.einsum('hqk,khd->qhd', dscores_wide, key_heads, precision=lax.Precision.HIGHEST) * inv_root).astype(jnp.bfloat16).reshape(span, H * HD)
    shards = span // TOK_DEV
    dscore_shards = dscores_wide.reshape(H, shards, TOK_DEV, span)
    prob_shards = probs_low.astype(jnp.float32).reshape(H, shards, TOK_DEV, span)
    query_shards = query_heads.reshape(shards, TOK_DEV, H, HD)
    grad_shards = grad_heads.reshape(shards, TOK_DEV, H, HD)
    key_terms = (jnp.einsum('hsqk,sqhd->skhd', dscore_shards, query_shards, precision=lax.Precision.HIGHEST) * inv_root).astype(jnp.bfloat16)
    key_terms = lax.optimization_barrier(key_terms)
    key_grad = lax.optimization_barrier(jnp.sum(key_terms.astype(jnp.float32), axis=0)).astype(jnp.bfloat16).reshape(span, H * HD)
    value_terms = jnp.einsum('hsqk,sqhd->skhd', prob_shards, grad_shards, precision=lax.Precision.HIGHEST).astype(jnp.bfloat16)
    value_terms = lax.optimization_barrier(value_terms)
    value_grad = lax.optimization_barrier(jnp.sum(value_terms.astype(jnp.float32), axis=0)).astype(jnp.bfloat16).reshape(span, H * HD)
    return (query_grad, key_grad, value_grad)

def reference(queries, keys, values, out_grad, log_norm, row_delta, doc_lengths, bin_dest):
    span = 4 * TOK_DEV

    def per_bin(array):
        return array.reshape((ROWS * BINS, span) + array.shape[2:])
    packed = (per_bin(queries), per_bin(keys), per_bin(values), per_bin(out_grad), per_bin(log_norm), per_bin(row_delta), doc_lengths.reshape(ROWS * BINS, BIN_BLOCKS))
    home_q, home_k, home_v = lax.map(bin_backward, packed)
    row_index = jnp.arange(ROWS, dtype=jnp.int32)[:, None]
    partner = jnp.bitwise_xor(row_index, ROWS // 2)
    source_group = jnp.where(bin_dest != row_index, partner, row_index).astype(jnp.int32)
    flat_source = (source_group * BINS + jnp.arange(BINS, dtype=jnp.int32)[None, :]).reshape(-1).astype(jnp.int32)
    query_grad = jnp.take(home_q, flat_source, axis=0).reshape(ROWS, ROW, H * HD)
    key_grad = jnp.take(home_k, flat_source, axis=0).reshape(ROWS, ROW, H * HD)
    value_grad = jnp.take(home_v, flat_source, axis=0).reshape(ROWS, ROW, H * HD)
    return (query_grad, key_grad, value_grad)
```

```python
import functools
import math

import jax
import jax.numpy as jnp
from jax import lax
from jax.experimental import pallas as pl
from jax.experimental.pallas import tpu as pltpu
from jax.sharding import Mesh
from jax.sharding import PartitionSpec as P

TOK = 128
HEAD = 128
SIDES = 2
SPOTS = 4
TEAM = SIDES * SPOTS
STAT_ROWS = 16
IN_ROWS = 4 * TOK + STAT_ROWS
OUT_ROWS = 3 * TOK
MASKED = -1e30
ROOT = 1.0 / math.sqrt(HEAD)
LOG2E = math.log2(math.e)


def pack_kernel(q_ref, k_ref, v_ref, g_ref, norm_ref, delta_ref, out_ref, stats, sems, stat_sem):
    width = out_ref.shape[2]
    copies = []
    for member in range(TEAM):
        for slot, ref in enumerate((q_ref, k_ref, v_ref, g_ref)):
            copy = pltpu.make_async_copy(
                ref.at[0, :, pl.ds(member * width, width)],
                out_ref.at[member, pl.ds(slot * TOK, TOK), :],
                sems.at[member, slot],
            )
            copy.start()
            copies.append(copy)
    heads = norm_ref.shape[0]
    norm = norm_ref[...].astype(jnp.float32)
    delta = delta_ref[...].astype(jnp.float32)
    row = lax.broadcasted_iota(jnp.int32, (STAT_ROWS, HEAD), 0)
    per_member = heads // TEAM
    for head in range(heads):
        tile = jnp.where(row == 0, norm[head : head + 1], 0.0)
        tile = jnp.where(row == 1, delta[head : head + 1], tile)
        place = head % per_member * HEAD
        stats[head // per_member, :, place : place + HEAD] = tile.astype(jnp.bfloat16)
    copy = pltpu.make_async_copy(stats, out_ref.at[:, pl.ds(4 * TOK, STAT_ROWS), :], stat_sem)
    copy.start()
    copies.append(copy)
    for copy in copies:
        copy.wait()


def pack(q, k, v, g, norm, delta):
    width = q.shape[2] // TEAM
    anywhere = pl.BlockSpec(memory_space=pl.ANY)
    local = pl.BlockSpec(memory_space=pltpu.VMEM)
    return pl.pallas_call(
        pack_kernel,
        out_shape=jax.ShapeDtypeStruct((TEAM, IN_ROWS, width), jnp.bfloat16),
        in_specs=[anywhere] * 4 + [local] * 2,
        out_specs=anywhere,
        scratch_shapes=[
            pltpu.VMEM((TEAM, STAT_ROWS, width), jnp.bfloat16),
            pltpu.SemaphoreType.DMA((TEAM, 4)),
            pltpu.SemaphoreType.DMA,
        ],
        name="pack",
    )(q, k, v, g, norm, delta)


def nt(a, b):
    return lax.dot_general(a, b, (((1,), (1,)), ((), ())), preferred_element_type=jnp.float32)


def nn(a, b):
    return jnp.dot(a, b, preferred_element_type=jnp.float32)


def attend_kernel(swap_ref, docs_ref, in_ref, out_ref, ds_ref):
    side = pl.program_id(0)
    span = SPOTS * TOK

    def whole(slot):
        return in_ref[:, slot * TOK : (slot + 1) * TOK, :].reshape(span, HEAD)

    q, k, v, g = (whole(slot) for slot in range(4))
    stats = [in_ref[spot, 4 * TOK :, :].astype(jnp.float32) for spot in range(SPOTS)]
    delta = jnp.concatenate([stat[1:2] for stat in stats], axis=1)
    for key_spot in range(SPOTS):
        rows = slice(key_spot * TOK, (key_spot + 1) * TOK)
        key_doc = docs_ref[side, key_spot]
        bias = jnp.concatenate(
            [
                jnp.where(docs_ref[side, spot] == key_doc, stats[spot][0:1] * -LOG2E, MASKED)
                for spot in range(SPOTS)
            ],
            axis=1,
        )
        probs = jnp.exp2(nt(k[rows], q) * (ROOT * LOG2E) + bias)
        dscores = (probs * (nt(v[rows], g) - delta)).astype(jnp.bfloat16)
        ds_ref[rows, :] = dscores
        out_ref[key_spot, TOK : 2 * TOK, :] = (nn(dscores, q) * ROOT).astype(jnp.bfloat16)
        out_ref[key_spot, 2 * TOK :, :] = nn(probs.astype(jnp.bfloat16), g).astype(jnp.bfloat16)
    dq = (nn(k.T, ds_ref[...]) * ROOT).T.astype(jnp.bfloat16)
    for spot in range(SPOTS):
        out_ref[spot, :TOK, :] = dq[spot * TOK : (spot + 1) * TOK]


def attend(swap, docs, messages):
    per_member = messages.shape[2] // HEAD
    return pl.pallas_call(
        attend_kernel,
        out_shape=jax.ShapeDtypeStruct((TEAM, OUT_ROWS, per_member * HEAD), jnp.bfloat16),
        grid_spec=pltpu.PrefetchScalarGridSpec(
            num_scalar_prefetch=2,
            grid=(SIDES, per_member),
            in_specs=[
                pl.BlockSpec((SPOTS, IN_ROWS, HEAD), lambda side, head, swap, docs: (side, 0, head))
            ],
            out_specs=pl.BlockSpec(
                (SPOTS, OUT_ROWS, HEAD),
                lambda side, head, swap, docs: (jnp.bitwise_xor(side, swap[0]), 0, head),
            ),
            scratch_shapes=[pltpu.VMEM((SPOTS * TOK, SPOTS * TOK), jnp.bfloat16)],
        ),
        name="attend",
    )(swap, docs, messages)


def unpack_kernel(in_ref, q_ref, k_ref, v_ref, sems):
    width = in_ref.shape[2]
    copies = []
    for member in range(TEAM):
        for slot, ref in enumerate((q_ref, k_ref, v_ref)):
            copy = pltpu.make_async_copy(
                in_ref.at[member, pl.ds(slot * TOK, TOK), :],
                ref.at[0, :, pl.ds(member * width, width)],
                sems.at[member, slot],
            )
            copy.start()
            copies.append(copy)
    for copy in copies:
        copy.wait()


def unpack(messages):
    anywhere = pl.BlockSpec(memory_space=pl.ANY)
    shape = jax.ShapeDtypeStruct((1, TOK, TEAM * messages.shape[2]), jnp.bfloat16)
    return pl.pallas_call(
        unpack_kernel,
        out_shape=(shape,) * 3,
        in_specs=[anywhere],
        out_specs=(anywhere,) * 3,
        scratch_shapes=[pltpu.SemaphoreType.DMA((TEAM, 3))],
        name="unpack",
    )(messages)


def body(q, k, v, g, norm, delta, doc_lengths, bin_dest):
    groups = lax.axis_size("low")
    low = lax.axis_index("low")
    bin_index = lax.axis_index("bin")
    swap = (bin_dest[low, bin_index] != low).astype(jnp.int32)[None]
    lengths = doc_lengths.reshape((SIDES, groups) + doc_lengths.shape[1:])[:, low, bin_index]
    ends = jnp.cumsum(lengths, axis=1)
    docs = jnp.sum(
        (ends[:, None, :] <= jnp.arange(SPOTS, dtype=jnp.int32)[None, :, None]).astype(jnp.int32),
        axis=2,
    )
    team = ("side", "spot")
    packed = pack(q, k, v, g, jnp.transpose(norm[0]), jnp.transpose(delta[0]))
    messages = lax.all_to_all(packed, team, 0, 0, tiled=True)
    grads = lax.all_to_all(attend(swap, docs, messages), team, 0, 0, tiled=True)
    return unpack(grads)


def solution(mesh):
    dp, ctx = mesh.devices.shape
    fine = Mesh(
        mesh.devices.reshape(SIDES, dp // SIDES, ctx // SPOTS, SPOTS),
        ("side", "low", "bin", "spot"),
    )
    split = P(("side", "low"), ("bin", "spot"), None)
    return jax.shard_map(
        body,
        mesh=fine,
        in_specs=(split,) * 6 + (P(), P()),
        out_specs=(split,) * 3,
        check_vma=False,
    )
```

```python
import math

import jax
import jax.numpy as jnp
from jax import lax
from jax.experimental import pallas as pl
from jax.experimental.pallas import tpu as pltpu
from jax.sharding import Mesh
from jax.sharding import PartitionSpec as P

TOK = 128
HEAD = 128
SIDES = 2
SPOTS = 4
TEAM = SIDES * SPOTS
STAT_ROWS = 16
IN_ROWS = 4 * TOK + STAT_ROWS
OUT_ROWS = 3 * TOK
PACK_STEPS = 4
MASKED = -1e30
ROOT = 1.0 / math.sqrt(HEAD)
LOG2E = math.log2(math.e)


def pack_kernel(q_ref, k_ref, v_ref, g_ref, norm_ref, delta_ref, out_ref):
    members, _, width = out_ref.shape
    step = pl.program_id(0)
    row = lax.broadcasted_iota(jnp.int32, (STAT_ROWS, HEAD), 0)
    per_member = width // HEAD
    norm = norm_ref[...].astype(jnp.float32)
    delta = delta_ref[...].astype(jnp.float32)
    head_row = lax.broadcasted_iota(jnp.int32, norm.shape, 0)
    for member in range(members):
        for slot, ref in enumerate((q_ref, k_ref, v_ref, g_ref)):
            out_ref[member, slot * TOK : (slot + 1) * TOK, :] = ref[
                0, :, member * width : (member + 1) * width
            ]
        for place in range(per_member):
            here = head_row == (step * members + member) * per_member + place
            head_norm = jnp.sum(jnp.where(here, norm, 0.0), axis=0, keepdims=True)
            head_delta = jnp.sum(jnp.where(here, delta, 0.0), axis=0, keepdims=True)
            tile = jnp.where(row == 0, head_norm, jnp.where(row == 1, head_delta, 0.0))
            out_ref[member, 4 * TOK :, place * HEAD : (place + 1) * HEAD] = tile.astype(
                jnp.bfloat16
            )


def pack(q, k, v, g, norm, delta):
    width = q.shape[2] // TEAM
    members = TEAM // PACK_STEPS
    columns = pl.BlockSpec((1, TOK, members * width), lambda step: (0, 0, step))
    stats = pl.BlockSpec(norm.shape, lambda step: (0, 0))
    return pl.pallas_call(
        pack_kernel,
        out_shape=jax.ShapeDtypeStruct((TEAM, IN_ROWS, width), jnp.bfloat16),
        grid=(PACK_STEPS,),
        in_specs=[columns] * 4 + [stats] * 2,
        out_specs=pl.BlockSpec((members, IN_ROWS, width), lambda step: (step, 0, 0)),
        name="pack",
    )(q, k, v, g, norm, delta)


def nt(a, b):
    return lax.dot_general(a, b, (((1,), (1,)), ((), ())), preferred_element_type=jnp.float32)


def nn(a, b):
    return jnp.dot(a, b, preferred_element_type=jnp.float32)


def attend_kernel(swap_ref, docs_ref, in_ref, out_ref, ds_ref):
    side = pl.program_id(0)
    span = SPOTS * TOK

    def whole(slot):
        return in_ref[:, slot * TOK : (slot + 1) * TOK, :].reshape(span, HEAD)

    q, k, v, g = (whole(slot) for slot in range(4))
    stats = [in_ref[spot, 4 * TOK :, :].astype(jnp.float32) for spot in range(SPOTS)]
    delta = jnp.concatenate([stat[1:2] for stat in stats], axis=1)
    for key_spot in range(SPOTS):
        rows = slice(key_spot * TOK, (key_spot + 1) * TOK)
        key_doc = docs_ref[side, key_spot]
        bias = jnp.concatenate(
            [
                jnp.where(docs_ref[side, spot] == key_doc, stats[spot][0:1] * -LOG2E, MASKED)
                for spot in range(SPOTS)
            ],
            axis=1,
        )
        probs = jnp.exp2(nt(k[rows], q) * (ROOT * LOG2E) + bias)
        dscores = (probs * (nt(v[rows], g) - delta)).astype(jnp.bfloat16)
        ds_ref[rows, :] = dscores
        out_ref[key_spot, TOK : 2 * TOK, :] = (nn(dscores, q) * ROOT).astype(jnp.bfloat16)
        out_ref[key_spot, 2 * TOK :, :] = nn(probs.astype(jnp.bfloat16), g).astype(jnp.bfloat16)
    dq = (nn(k.T, ds_ref[...]) * ROOT).T.astype(jnp.bfloat16)
    for spot in range(SPOTS):
        out_ref[spot, :TOK, :] = dq[spot * TOK : (spot + 1) * TOK]


def attend(swap, docs, messages):
    per_member = messages.shape[2] // HEAD
    return pl.pallas_call(
        attend_kernel,
        out_shape=jax.ShapeDtypeStruct((TEAM, OUT_ROWS, per_member * HEAD), jnp.bfloat16),
        grid_spec=pltpu.PrefetchScalarGridSpec(
            num_scalar_prefetch=2,
            grid=(SIDES, per_member),
            in_specs=[
                pl.BlockSpec((SPOTS, IN_ROWS, HEAD), lambda side, head, swap, docs: (side, 0, head))
            ],
            out_specs=pl.BlockSpec(
                (SPOTS, OUT_ROWS, HEAD),
                lambda side, head, swap, docs: (jnp.bitwise_xor(side, swap[0]), 0, head),
            ),
            scratch_shapes=[pltpu.VMEM((SPOTS * TOK, SPOTS * TOK), jnp.bfloat16)],
        ),
        name="attend",
    )(swap, docs, messages)


def unpack_kernel(in_ref, q_ref, k_ref, v_ref):
    members, _, width = in_ref.shape
    for member in range(members):
        for slot, ref in enumerate((q_ref, k_ref, v_ref)):
            ref[0, :, member * width : (member + 1) * width] = in_ref[
                member, slot * TOK : (slot + 1) * TOK, :
            ]


def unpack(messages):
    width = messages.shape[2]
    members = TEAM // PACK_STEPS
    columns = pl.BlockSpec((1, TOK, members * width), lambda step: (0, 0, step))
    return pl.pallas_call(
        unpack_kernel,
        out_shape=(jax.ShapeDtypeStruct((1, TOK, TEAM * width), jnp.bfloat16),) * 3,
        grid=(PACK_STEPS,),
        in_specs=[pl.BlockSpec((members, OUT_ROWS, width), lambda step: (step, 0, 0))],
        out_specs=(columns,) * 3,
        name="unpack",
    )(messages)


def body(q, k, v, g, norm, delta, doc_lengths, bin_dest):
    groups = lax.axis_size("low")
    low = lax.axis_index("low")
    bin_index = lax.axis_index("bin")
    swap = (bin_dest[low, bin_index] != low).astype(jnp.int32)[None]
    lengths = doc_lengths.reshape((SIDES, groups) + doc_lengths.shape[1:])[:, low, bin_index]
    ends = jnp.cumsum(lengths, axis=1)
    docs = jnp.sum(
        (ends[:, None, :] <= jnp.arange(SPOTS, dtype=jnp.int32)[None, :, None]).astype(jnp.int32),
        axis=2,
    )
    team = ("side", "spot")
    packed = pack(q, k, v, g, jnp.transpose(norm[0]), jnp.transpose(delta[0]))
    messages = lax.all_to_all(packed, team, 0, 0, tiled=True)
    grads = lax.all_to_all(attend(swap, docs, messages), team, 0, 0, tiled=True)
    return unpack(grads)


def solution(mesh):
    dp, ctx = mesh.devices.shape
    fine = Mesh(
        mesh.devices.reshape(SIDES, dp // SIDES, ctx // SPOTS, SPOTS),
        ("side", "low", "bin", "spot"),
    )
    split = P(("side", "low"), ("bin", "spot"), None)
    return jax.shard_map(
        body,
        mesh=fine,
        in_specs=(split,) * 6 + (P(), P()),
        out_specs=(split,) * 3,
        check_vma=False,
    )
```

```python
import math

import jax
import jax.numpy as jnp
from jax import lax
from jax.experimental import pallas as pl
from jax.experimental.pallas import tpu as pltpu
from jax.sharding import Mesh
from jax.sharding import PartitionSpec as P

TOK = 128
HEAD = 128
SIDES = 2
SPOTS = 4
TEAM = SIDES * SPOTS
STAT_ROWS = 16
IN_ROWS = 4 * TOK + STAT_ROWS
OUT_ROWS = 3 * TOK
MASKED = -1e30
ROOT = 1.0 / math.sqrt(HEAD)
LOG2E = math.log2(math.e)
VMEM_LIMIT = 24 << 20


def start_all(copies):
    for copy in copies:
        copy.start()
    return copies


def pack_kernel(q_ref, k_ref, v_ref, g_ref, norm_ref, delta_ref, out_ref, stats, sems, stat_sems):
    width = out_ref.shape[2]
    stat_copies = start_all(
        [
            pltpu.make_async_copy(ref, stats.at[slot], stat_sems.at[slot])
            for slot, ref in enumerate((norm_ref, delta_ref))
        ]
    )
    copies = start_all(
        [
            pltpu.make_async_copy(
                ref.at[0, :, pl.ds(member * width, width)],
                out_ref.at[member, pl.ds(slot * TOK, TOK), :],
                sems.at[member, slot],
            )
            for member in range(TEAM)
            for slot, ref in enumerate((q_ref, k_ref, v_ref, g_ref))
        ]
    )
    for copy in stat_copies:
        copy.wait()
    norm = stats[0].astype(jnp.float32)
    delta = stats[1].astype(jnp.float32)
    row = lax.broadcasted_iota(jnp.int32, (STAT_ROWS, HEAD), 0)
    per_member = width // HEAD
    for head in range(TEAM * per_member):
        tile = jnp.where(row == 0, norm[head : head + 1], 0.0)
        tile = jnp.where(row == 1, delta[head : head + 1], tile)
        place = head % per_member * HEAD
        out_ref[head // per_member, 4 * TOK :, place : place + HEAD] = tile.astype(jnp.bfloat16)
    for copy in copies:
        copy.wait()


def in_hbm(array):
    return pltpu.with_memory_space_constraint(array, pltpu.HBM)


def in_vmem(array):
    return pltpu.with_memory_space_constraint(array, pltpu.VMEM)


ANYWHERE = pl.BlockSpec(memory_space=pl.ANY)
LOCAL = pl.BlockSpec(memory_space=pltpu.VMEM)
PARAMS = pltpu.CompilerParams(vmem_limit_bytes=VMEM_LIMIT)


def pack(q, k, v, g, norm, delta):
    width = q.shape[2] // TEAM
    return pl.pallas_call(
        pack_kernel,
        out_shape=pltpu.VMEM((TEAM, IN_ROWS, width), jnp.bfloat16),
        in_specs=[ANYWHERE] * 6,
        out_specs=LOCAL,
        scratch_shapes=[
            pltpu.VMEM((2,) + norm.shape, jnp.bfloat16),
            pltpu.SemaphoreType.DMA((TEAM, 4)),
            pltpu.SemaphoreType.DMA((2,)),
        ],
        compiler_params=PARAMS,
        name="pack",
    )(*(in_hbm(array) for array in (q, k, v, g, norm, delta)))


def nt(a, b):
    return lax.dot_general(a, b, (((1,), (1,)), ((), ())), preferred_element_type=jnp.float32)


def nn(a, b):
    return jnp.dot(a, b, preferred_element_type=jnp.float32)


def attend_kernel(swap_ref, docs_ref, in_ref, out_ref, ds_ref):
    span = SPOTS * TOK
    per_member = in_ref.shape[2] // HEAD
    swap = swap_ref[0]

    @pl.loop(0, SIDES * per_member)
    def unit(index):
        side = index // per_member
        lanes = pl.ds(pl.multiple_of(index % per_member * HEAD, HEAD), HEAD)
        source = pl.ds(side * SPOTS, SPOTS)
        target = jnp.bitwise_xor(side, swap) * SPOTS

        def whole(slot):
            return in_ref[source, slot * TOK : (slot + 1) * TOK, lanes].reshape(span, HEAD)

        q, k, v, g = (whole(slot) for slot in range(4))
        stats = [
            in_ref[side * SPOTS + spot, 4 * TOK :, lanes].astype(jnp.float32)
            for spot in range(SPOTS)
        ]
        delta = jnp.concatenate([stat[1:2] for stat in stats], axis=1)
        for key_spot in range(SPOTS):
            rows = slice(key_spot * TOK, (key_spot + 1) * TOK)
            key_doc = docs_ref[side, key_spot]
            bias = jnp.concatenate(
                [
                    jnp.where(docs_ref[side, spot] == key_doc, stats[spot][0:1] * -LOG2E, MASKED)
                    for spot in range(SPOTS)
                ],
                axis=1,
            )
            probs = jnp.exp2(nt(k[rows], q) * (ROOT * LOG2E) + bias)
            dscores = (probs * (nt(v[rows], g) - delta)).astype(jnp.bfloat16)
            ds_ref[rows, :] = dscores
            out_ref[target + key_spot, TOK : 2 * TOK, lanes] = (nn(dscores, q) * ROOT).astype(
                jnp.bfloat16
            )
            out_ref[target + key_spot, 2 * TOK :, lanes] = nn(probs.astype(jnp.bfloat16), g).astype(
                jnp.bfloat16
            )
        dq = (nn(k.T, ds_ref[...]) * ROOT).T.astype(jnp.bfloat16)
        for spot in range(SPOTS):
            out_ref[target + spot, :TOK, lanes] = dq[spot * TOK : (spot + 1) * TOK]


def attend(swap, docs, messages):
    span = SPOTS * TOK
    units = SIDES * messages.shape[2] // HEAD
    scalars = pl.BlockSpec(memory_space=pltpu.SMEM)
    return pl.pallas_call(
        attend_kernel,
        out_shape=pltpu.VMEM((TEAM, OUT_ROWS, messages.shape[2]), jnp.bfloat16),
        in_specs=[scalars, scalars, LOCAL],
        out_specs=LOCAL,
        scratch_shapes=[pltpu.VMEM((span, span), jnp.bfloat16)],
        compiler_params=PARAMS,
        cost_estimate=pl.CostEstimate(
            flops=units * 10 * span * span * HEAD,
            bytes_accessed=4 << 20,
            transcendentals=units * span * span,
        ),
        name="attend",
    )(swap, docs, in_vmem(messages))


def unpack_kernel(in_ref, q_ref, k_ref, v_ref, sems):
    width = in_ref.shape[2]
    copies = start_all(
        [
            pltpu.make_async_copy(
                in_ref.at[member, pl.ds(slot * TOK, TOK), :],
                ref.at[0, :, pl.ds(member * width, width)],
                sems.at[member, slot],
            )
            for member in range(TEAM)
            for slot, ref in enumerate((q_ref, k_ref, v_ref))
        ]
    )
    for copy in copies:
        copy.wait()


def unpack(messages):
    shape = (1, TOK, TEAM * messages.shape[2])
    return pl.pallas_call(
        unpack_kernel,
        out_shape=(pltpu.HBM(shape, jnp.bfloat16),) * 3,
        in_specs=[LOCAL],
        out_specs=(ANYWHERE,) * 3,
        scratch_shapes=[pltpu.SemaphoreType.DMA((TEAM, 3))],
        compiler_params=PARAMS,
        name="unpack",
    )(in_vmem(messages))


def body(q, k, v, g, norm, delta, doc_lengths, bin_dest):
    groups = lax.axis_size("low")
    low = lax.axis_index("low")
    bin_index = lax.axis_index("bin")
    swap = (bin_dest[low, bin_index] != low).astype(jnp.int32)[None]
    lengths = doc_lengths.reshape((SIDES, groups) + doc_lengths.shape[1:])[:, low, bin_index]
    ends = jnp.cumsum(lengths, axis=1)
    docs = jnp.sum(
        (ends[:, None, :] <= jnp.arange(SPOTS, dtype=jnp.int32)[None, :, None]).astype(jnp.int32),
        axis=2,
    )
    team = ("side", "spot")
    packed = pack(q, k, v, g, jnp.transpose(norm[0]), jnp.transpose(delta[0]))
    messages = lax.all_to_all(packed, team, 0, 0, tiled=True)
    grads = lax.all_to_all(attend(swap, docs, messages), team, 0, 0, tiled=True)
    return unpack(grads)


def solution(mesh):
    dp, ctx = mesh.devices.shape
    fine = Mesh(
        mesh.devices.reshape(SIDES, dp // SIDES, ctx // SPOTS, SPOTS),
        ("side", "low", "bin", "spot"),
    )
    split = P(("side", "low"), ("bin", "spot"), None)
    return jax.shard_map(
        body,
        mesh=fine,
        in_specs=(split,) * 6 + (P(), P()),
        out_specs=(split,) * 3,
        check_vma=False,
    )
```

```python
import math

import jax
import jax.numpy as jnp
from jax import lax
from jax.experimental import pallas as pl
from jax.experimental.pallas import tpu as pltpu
from jax.sharding import Mesh
from jax.sharding import PartitionSpec as P

TOK = 128
HEAD = 128
SIDES = 2
SPOTS = 4
TEAM = SIDES * SPOTS
STAT_ROWS = 16
IN_ROWS = 4 * TOK + STAT_ROWS
OUT_ROWS = 3 * TOK
MASKED = -1e30
ROOT = 1.0 / math.sqrt(HEAD)
LOG2E = math.log2(math.e)
QUERY_SPOTS = 4
VMEM_LIMIT = 24 << 20


def start_all(copies):
    for copy in copies:
        copy.start()
    return copies


def pack_kernel(q_ref, k_ref, v_ref, g_ref, norm_ref, delta_ref, out_ref, held, stats, sems, stat_sems):
    width = out_ref.shape[2]
    stat_copies = start_all(
        [
            pltpu.make_async_copy(ref, stats.at[slot], stat_sems.at[slot])
            for slot, ref in enumerate((norm_ref, delta_ref))
        ]
    )
    copies = start_all(
        [
            pltpu.make_async_copy(ref.at[0], held.at[slot], sems.at[slot])
            for slot, ref in enumerate((q_ref, k_ref, v_ref, g_ref))
        ]
    )
    for copy in stat_copies:
        copy.wait()
    norm = stats[0].astype(jnp.float32)
    delta = stats[1].astype(jnp.float32)
    row = lax.broadcasted_iota(jnp.int32, (STAT_ROWS, HEAD), 0)
    per_member = width // HEAD
    for head in range(TEAM * per_member):
        tile = jnp.where(row == 0, norm[head : head + 1], 0.0)
        tile = jnp.where(row == 1, delta[head : head + 1], tile)
        place = head % per_member * HEAD
        out_ref[head // per_member, 4 * TOK :, place : place + HEAD] = tile.astype(jnp.bfloat16)
    for slot, copy in enumerate(copies):
        copy.wait()
        for member in range(TEAM):
            out_ref[member, slot * TOK : (slot + 1) * TOK, :] = held[
                slot, :, member * width : (member + 1) * width
            ]


def in_hbm(array):
    return pltpu.with_memory_space_constraint(array, pltpu.HBM)


def in_vmem(array):
    return pltpu.with_memory_space_constraint(array, pltpu.VMEM)


ANYWHERE = pl.BlockSpec(memory_space=pl.ANY)
LOCAL = pl.BlockSpec(memory_space=pltpu.VMEM)
PARAMS = pltpu.CompilerParams(vmem_limit_bytes=VMEM_LIMIT)


def pack(q, k, v, g, norm, delta):
    width = q.shape[2] // TEAM
    return pl.pallas_call(
        pack_kernel,
        out_shape=pltpu.VMEM((TEAM, IN_ROWS, width), jnp.bfloat16),
        in_specs=[ANYWHERE] * 6,
        out_specs=LOCAL,
        scratch_shapes=[
            pltpu.VMEM((4,) + q.shape[1:], jnp.bfloat16),
            pltpu.VMEM((2,) + norm.shape, jnp.bfloat16),
            pltpu.SemaphoreType.DMA((4,)),
            pltpu.SemaphoreType.DMA((2,)),
        ],
        compiler_params=PARAMS,
        name="pack",
    )(*(in_hbm(array) for array in (q, k, v, g, norm, delta)))


def nt(a, b):
    return lax.dot_general(a, b, (((1,), (1,)), ((), ())), preferred_element_type=jnp.float32)


def nn(a, b):
    return jnp.dot(a, b, preferred_element_type=jnp.float32)


def attend_kernel(swap_ref, docs_ref, in_ref, out_ref):
    span = SPOTS * TOK
    per_member = in_ref.shape[2] // HEAD
    swap = swap_ref[0]

    def unit(side, lanes):
        source = slice(side * SPOTS, (side + 1) * SPOTS)
        target = jnp.bitwise_xor(side, swap) * SPOTS

        def whole(slot):
            return in_ref[source, slot * TOK : (slot + 1) * TOK, lanes].reshape(span, HEAD)

        q, k, v, g = (whole(slot) for slot in range(4))
        k_turned = k.T
        dk = jnp.zeros((span, HEAD), jnp.float32)
        dv = jnp.zeros((span, HEAD), jnp.float32)
        for first in range(0, SPOTS, QUERY_SPOTS):
            spots = range(first, first + QUERY_SPOTS)
            columns = slice(first * TOK, (first + QUERY_SPOTS) * TOK)
            stats = [
                in_ref[side * SPOTS + spot, 4 * TOK :, lanes].astype(jnp.float32)
                for spot in spots
            ]
            delta = jnp.concatenate([stat[1:2] for stat in stats], axis=1)
            scores = nt(k, q[columns])
            dprobs = nt(v, g[columns])
            probs_low, dscores = [], []
            for key_spot in range(SPOTS):
                rows = slice(key_spot * TOK, (key_spot + 1) * TOK)
                key_doc = docs_ref[side, key_spot]
                bias = jnp.concatenate(
                    [
                        jnp.where(docs_ref[side, spot] == key_doc, stat[0:1] * -LOG2E, MASKED)
                        for spot, stat in zip(spots, stats)
                    ],
                    axis=1,
                )
                probs = jnp.exp2(scores[rows] * (ROOT * LOG2E) + bias)
                probs_low.append(probs.astype(jnp.bfloat16))
                dscores.append((probs * (dprobs[rows] - delta)).astype(jnp.bfloat16))
            probs_low = jnp.concatenate(probs_low, axis=0)
            dscores = jnp.concatenate(dscores, axis=0)
            dk = dk + nn(dscores, q[columns])
            dv = dv + nn(probs_low, g[columns])
            dq = (nn(k_turned, dscores) * ROOT).T.astype(jnp.bfloat16)
            for place, spot in enumerate(spots):
                out_ref[target + spot, :TOK, lanes] = dq[place * TOK : (place + 1) * TOK]
        dk = (dk * ROOT).astype(jnp.bfloat16)
        dv = dv.astype(jnp.bfloat16)
        for spot in range(SPOTS):
            rows = slice(spot * TOK, (spot + 1) * TOK)
            out_ref[target + spot, TOK : 2 * TOK, lanes] = dk[rows]
            out_ref[target + spot, 2 * TOK :, lanes] = dv[rows]

    for side in range(SIDES):
        for head in range(per_member):
            unit(side, slice(head * HEAD, (head + 1) * HEAD))


def attend(swap, docs, messages):
    span = SPOTS * TOK
    units = SIDES * messages.shape[2] // HEAD
    scalars = pl.BlockSpec(memory_space=pltpu.SMEM)
    return pl.pallas_call(
        attend_kernel,
        out_shape=pltpu.VMEM((TEAM, OUT_ROWS, messages.shape[2]), jnp.bfloat16),
        in_specs=[scalars, scalars, LOCAL],
        out_specs=LOCAL,
        compiler_params=PARAMS,
        cost_estimate=pl.CostEstimate(
            flops=units * 10 * span * span * HEAD,
            bytes_accessed=4 << 20,
            transcendentals=units * span * span,
        ),
        name="attend",
    )(swap, docs, in_vmem(messages))


def unpack_kernel(in_ref, q_ref, k_ref, v_ref, sems):
    width = in_ref.shape[2]
    copies = start_all(
        [
            pltpu.make_async_copy(
                in_ref.at[member, pl.ds(slot * TOK, TOK), :],
                ref.at[0, :, pl.ds(member * width, width)],
                sems.at[member, slot],
            )
            for member in range(TEAM)
            for slot, ref in enumerate((q_ref, k_ref, v_ref))
        ]
    )
    for copy in copies:
        copy.wait()


def unpack(messages):
    shape = (1, TOK, TEAM * messages.shape[2])
    return pl.pallas_call(
        unpack_kernel,
        out_shape=(pltpu.HBM(shape, jnp.bfloat16),) * 3,
        in_specs=[LOCAL],
        out_specs=(ANYWHERE,) * 3,
        scratch_shapes=[pltpu.SemaphoreType.DMA((TEAM, 3))],
        compiler_params=PARAMS,
        name="unpack",
    )(in_vmem(messages))


def body(q, k, v, g, norm, delta, doc_lengths, bin_dest):
    groups = lax.axis_size("low")
    low = lax.axis_index("low")
    bin_index = lax.axis_index("bin")
    swap = (bin_dest[low, bin_index] != low).astype(jnp.int32)[None]
    lengths = doc_lengths.reshape((SIDES, groups) + doc_lengths.shape[1:])[:, low, bin_index]
    ends = jnp.cumsum(lengths, axis=1)
    docs = jnp.sum(
        (ends[:, None, :] <= jnp.arange(SPOTS, dtype=jnp.int32)[None, :, None]).astype(jnp.int32),
        axis=2,
    )
    team = ("side", "spot")
    packed = pack(q, k, v, g, jnp.transpose(norm[0]), jnp.transpose(delta[0]))
    messages = lax.all_to_all(packed, team, 0, 0, tiled=True)
    grads = lax.all_to_all(attend(swap, docs, messages), team, 0, 0, tiled=True)
    return unpack(grads)


def solution(mesh):
    dp, ctx = mesh.devices.shape
    fine = Mesh(
        mesh.devices.reshape(SIDES, dp // SIDES, ctx // SPOTS, SPOTS),
        ("side", "low", "bin", "spot"),
    )
    split = P(("side", "low"), ("bin", "spot"), None)
    return jax.shard_map(
        body,
        mesh=fine,
        in_specs=(split,) * 6 + (P(), P()),
        out_specs=(split,) * 3,
        check_vma=False,
    )
```

```python
import math

import jax
import jax.numpy as jnp
from jax import lax
from jax.experimental import pallas as pl
from jax.experimental.pallas import tpu as pltpu
from jax.sharding import Mesh
from jax.sharding import PartitionSpec as P

TOK = 128
HEAD = 128
SIDES = 2
SPOTS = 4
TEAM = SIDES * SPOTS
ORDER = (0, 2, 1, 3, 5, 7, 4, 6)
STAT_ROWS = 16
IN_ROWS = 4 * TOK + STAT_ROWS
OUT_ROWS = 3 * TOK
MASKED = -1e30
ROOT = 1.0 / math.sqrt(HEAD)
LOG2E = math.log2(math.e)
QUERY_SPOTS = 4
VMEM_LIMIT = 24 << 20


def start_all(copies):
    for copy in copies:
        copy.start()
    return copies


def pack_kernel(q_ref, k_ref, v_ref, g_ref, norm_ref, delta_ref, out_ref, held, stats, sems, stat_sems):
    width = out_ref.shape[2]
    stat_copies = start_all(
        [
            pltpu.make_async_copy(ref, stats.at[slot], stat_sems.at[slot])
            for slot, ref in enumerate((norm_ref, delta_ref))
        ]
    )
    copies = start_all(
        [
            pltpu.make_async_copy(ref.at[0], held.at[slot], sems.at[slot])
            for slot, ref in enumerate((q_ref, k_ref, v_ref, g_ref))
        ]
    )
    for copy in stat_copies:
        copy.wait()
    norm = stats[0].astype(jnp.float32)
    delta = stats[1].astype(jnp.float32)
    row = lax.broadcasted_iota(jnp.int32, (STAT_ROWS, HEAD), 0)
    per_member = width // HEAD
    for head in range(TEAM * per_member):
        tile = jnp.where(row == 0, norm[head : head + 1], 0.0)
        tile = jnp.where(row == 1, delta[head : head + 1], tile)
        place = head % per_member * HEAD
        out_ref[head // per_member, 4 * TOK :, place : place + HEAD] = tile.astype(jnp.bfloat16)
    for slot, copy in enumerate(copies):
        copy.wait()
        for member in range(TEAM):
            out_ref[member, slot * TOK : (slot + 1) * TOK, :] = held[
                slot, :, member * width : (member + 1) * width
            ]


def in_hbm(array):
    return pltpu.with_memory_space_constraint(array, pltpu.HBM)


def in_vmem(array):
    return pltpu.with_memory_space_constraint(array, pltpu.VMEM)


ANYWHERE = pl.BlockSpec(memory_space=pl.ANY)
LOCAL = pl.BlockSpec(memory_space=pltpu.VMEM)
PARAMS = pltpu.CompilerParams(vmem_limit_bytes=VMEM_LIMIT)


def pack(q, k, v, g, norm, delta):
    width = q.shape[2] // TEAM
    return pl.pallas_call(
        pack_kernel,
        out_shape=pltpu.VMEM((TEAM, IN_ROWS, width), jnp.bfloat16),
        in_specs=[ANYWHERE] * 6,
        out_specs=LOCAL,
        scratch_shapes=[
            pltpu.VMEM((4,) + q.shape[1:], jnp.bfloat16),
            pltpu.VMEM((2,) + norm.shape, jnp.bfloat16),
            pltpu.SemaphoreType.DMA((4,)),
            pltpu.SemaphoreType.DMA((2,)),
        ],
        compiler_params=PARAMS,
        name="pack",
    )(*(in_hbm(array) for array in (q, k, v, g, norm, delta)))


def nt(a, b):
    return lax.dot_general(a, b, (((1,), (1,)), ((), ())), preferred_element_type=jnp.float32)


def nn(a, b):
    return jnp.dot(a, b, preferred_element_type=jnp.float32)


def message_of(member):
    return jnp.bitwise_xor(ORDER.index(member), (TEAM - 1) * (lax.axis_index("low") % 2))


def attend_kernel(swap_ref, docs_ref, in_ref, out_ref):
    span = SPOTS * TOK
    per_member = in_ref.shape[2] // HEAD
    swapped = swap_ref[0] != 0
    places = [message_of(member) for member in range(TEAM)]

    def unit(side, lanes):
        own = places[side * SPOTS : (side + 1) * SPOTS]
        other = places[(1 - side) * SPOTS : (2 - side) * SPOTS]
        target = [jnp.where(swapped, theirs, ours) for ours, theirs in zip(own, other)]

        def whole(slot):
            rows = slice(slot * TOK, (slot + 1) * TOK)
            return jnp.concatenate([in_ref[place, rows, lanes] for place in own], axis=0)

        q, k, v, g = (whole(slot) for slot in range(4))
        k_turned = k.T
        dk = jnp.zeros((span, HEAD), jnp.float32)
        dv = jnp.zeros((span, HEAD), jnp.float32)
        for first in range(0, SPOTS, QUERY_SPOTS):
            spots = range(first, first + QUERY_SPOTS)
            columns = slice(first * TOK, (first + QUERY_SPOTS) * TOK)
            stats = [
                in_ref[own[spot], 4 * TOK :, lanes].astype(jnp.float32)
                for spot in spots
            ]
            delta = jnp.concatenate([stat[1:2] for stat in stats], axis=1)
            scores = nt(k, q[columns])
            dprobs = nt(v, g[columns])
            probs_low, dscores = [], []
            for key_spot in range(SPOTS):
                rows = slice(key_spot * TOK, (key_spot + 1) * TOK)
                key_doc = docs_ref[side, key_spot]
                bias = jnp.concatenate(
                    [
                        jnp.where(docs_ref[side, spot] == key_doc, stat[0:1] * -LOG2E, MASKED)
                        for spot, stat in zip(spots, stats)
                    ],
                    axis=1,
                )
                probs = jnp.exp2(scores[rows] * (ROOT * LOG2E) + bias)
                probs_low.append(probs.astype(jnp.bfloat16))
                dscores.append((probs * (dprobs[rows] - delta)).astype(jnp.bfloat16))
            probs_low = jnp.concatenate(probs_low, axis=0)
            dscores = jnp.concatenate(dscores, axis=0)
            dk = dk + nn(dscores, q[columns])
            dv = dv + nn(probs_low, g[columns])
            dq = (nn(k_turned, dscores) * ROOT).T.astype(jnp.bfloat16)
            for place, spot in enumerate(spots):
                out_ref[target[spot], :TOK, lanes] = dq[place * TOK : (place + 1) * TOK]
        dk = (dk * ROOT).astype(jnp.bfloat16)
        dv = dv.astype(jnp.bfloat16)
        for spot in range(SPOTS):
            rows = slice(spot * TOK, (spot + 1) * TOK)
            out_ref[target[spot], TOK : 2 * TOK, lanes] = dk[rows]
            out_ref[target[spot], 2 * TOK :, lanes] = dv[rows]

    for side in range(SIDES):
        for head in range(per_member):
            unit(side, slice(head * HEAD, (head + 1) * HEAD))


def attend(swap, docs, messages):
    span = SPOTS * TOK
    units = SIDES * messages.shape[2] // HEAD
    scalars = pl.BlockSpec(memory_space=pltpu.SMEM)
    return pl.pallas_call(
        attend_kernel,
        out_shape=pltpu.VMEM((TEAM, OUT_ROWS, messages.shape[2]), jnp.bfloat16),
        in_specs=[scalars, scalars, LOCAL],
        out_specs=LOCAL,
        compiler_params=PARAMS,
        cost_estimate=pl.CostEstimate(
            flops=units * 10 * span * span * HEAD,
            bytes_accessed=4 << 20,
            transcendentals=units * span * span,
        ),
        name="attend",
    )(swap, docs, in_vmem(messages))


def unpack_kernel(in_ref, q_ref, k_ref, v_ref, sems):
    width = in_ref.shape[2]
    copies = start_all(
        [
            pltpu.make_async_copy(
                in_ref.at[member, pl.ds(slot * TOK, TOK), :],
                ref.at[0, :, pl.ds(member * width, width)],
                sems.at[member, slot],
            )
            for member in range(TEAM)
            for slot, ref in enumerate((q_ref, k_ref, v_ref))
        ]
    )
    for copy in copies:
        copy.wait()


def unpack(messages):
    shape = (1, TOK, TEAM * messages.shape[2])
    return pl.pallas_call(
        unpack_kernel,
        out_shape=(pltpu.HBM(shape, jnp.bfloat16),) * 3,
        in_specs=[LOCAL],
        out_specs=(ANYWHERE,) * 3,
        scratch_shapes=[pltpu.SemaphoreType.DMA((TEAM, 3))],
        compiler_params=PARAMS,
        name="unpack",
    )(in_vmem(messages))


def exchange(messages):
    axes = ("side", "low", "bin", "spot")
    _, lows, bins, _ = (lax.axis_size(axis) for axis in axes)
    teams = [
        [
            ((member // SPOTS * lows + low) * bins + place) * SPOTS + member % SPOTS
            for member in (ORDER[::-1] if low % 2 else ORDER)
        ]
        for low in range(lows)
        for place in range(bins)
    ]
    return lax.all_to_all(messages, axes, 0, 0, tiled=True, axis_index_groups=teams)


def body(q, k, v, g, norm, delta, doc_lengths, bin_dest):
    groups = lax.axis_size("low")
    low = lax.axis_index("low")
    bin_index = lax.axis_index("bin")
    swap = (bin_dest[low, bin_index] != low).astype(jnp.int32)[None]
    lengths = doc_lengths.reshape((SIDES, groups) + doc_lengths.shape[1:])[:, low, bin_index]
    ends = jnp.cumsum(lengths, axis=1)
    docs = jnp.sum(
        (ends[:, None, :] <= jnp.arange(SPOTS, dtype=jnp.int32)[None, :, None]).astype(jnp.int32),
        axis=2,
    )
    packed = pack(q, k, v, g, jnp.transpose(norm[0]), jnp.transpose(delta[0]))
    return unpack(exchange(attend(swap, docs, exchange(packed))))


def solution(mesh):
    dp, ctx = mesh.devices.shape
    fine = Mesh(
        mesh.devices.reshape(SIDES, dp // SIDES, ctx // SPOTS, SPOTS),
        ("side", "low", "bin", "spot"),
    )
    split = P(("side", "low"), ("bin", "spot"), None)
    return jax.shard_map(
        body,
        mesh=fine,
        in_specs=(split,) * 6 + (P(), P()),
        out_specs=(split,) * 3,
        check_vma=False,
    )
```

```python
import math

import jax
import jax.numpy as jnp
from jax import lax
from jax.experimental import pallas as pl
from jax.experimental.pallas import tpu as pltpu
from jax.sharding import Mesh
from jax.sharding import PartitionSpec as P

TOK = 128
HEAD = 128
SIDES = 2
SPOTS = 4
TEAM = SIDES * SPOTS
ORDERS = ((0, 2, 1, 3, 5, 7, 4, 6), (0, 4, 2, 6, 3, 7, 1, 5))
STAT_ROWS = 16
OUT_ROWS = 3 * TOK
MASKED = -1e30
ROOT = 1.0 / math.sqrt(HEAD)
LOG2E = math.log2(math.e)
QUERY_SPOTS = 4
VMEM_LIMIT = 24 << 20


def start_all(copies):
    for copy in copies:
        copy.start()
    return copies


def pack_kernel(q_ref, k_ref, v_ref, g_ref, norm_ref, delta_ref, out_ref, held, stats, sems, stat_sems):
    per_member = held.shape[2] // (TEAM * HEAD)
    stat_copies = start_all(
        [
            pltpu.make_async_copy(ref, stats.at[slot], stat_sems.at[slot])
            for slot, ref in enumerate((norm_ref, delta_ref))
        ]
    )
    copies = start_all(
        [
            pltpu.make_async_copy(ref.at[0], held.at[slot], sems.at[slot])
            for slot, ref in enumerate((q_ref, k_ref, v_ref, g_ref))
        ]
    )
    for copy in stat_copies:
        copy.wait()
    norm = stats[0].astype(jnp.float32)
    delta = stats[1].astype(jnp.float32)
    row = lax.broadcasted_iota(jnp.int32, (STAT_ROWS, HEAD), 0)
    for member in range(TEAM):
        tile = jnp.zeros((STAT_ROWS, HEAD), jnp.float32)
        for place in range(per_member):
            head = member * per_member + place
            tile = jnp.where(row == 2 * place, norm[head : head + 1], tile)
            tile = jnp.where(row == 2 * place + 1, delta[head : head + 1], tile)
        out_ref[member, per_member * 4 * TOK :, :] = tile.astype(jnp.bfloat16)
    for slot, copy in enumerate(copies):
        copy.wait()
        for head in range(TEAM * per_member):
            member, place = divmod(head, per_member)
            first = (place * 4 + slot) * TOK
            out_ref[member, first : first + TOK, :] = held[
                slot, :, head * HEAD : (head + 1) * HEAD
            ]


def in_hbm(array):
    return pltpu.with_memory_space_constraint(array, pltpu.HBM)


def in_vmem(array):
    return pltpu.with_memory_space_constraint(array, pltpu.VMEM)


ANYWHERE = pl.BlockSpec(memory_space=pl.ANY)
LOCAL = pl.BlockSpec(memory_space=pltpu.VMEM)
PARAMS = pltpu.CompilerParams(vmem_limit_bytes=VMEM_LIMIT)


def pack(q, k, v, g, norm, delta):
    rows = q.shape[2] // (TEAM * HEAD) * 4 * TOK + STAT_ROWS
    return pl.pallas_call(
        pack_kernel,
        out_shape=pltpu.VMEM((TEAM, rows, HEAD), jnp.bfloat16),
        in_specs=[ANYWHERE] * 6,
        out_specs=LOCAL,
        scratch_shapes=[
            pltpu.VMEM((4,) + q.shape[1:], jnp.bfloat16),
            pltpu.VMEM((2,) + norm.shape, jnp.bfloat16),
            pltpu.SemaphoreType.DMA((4,)),
            pltpu.SemaphoreType.DMA((2,)),
        ],
        compiler_params=PARAMS,
        name="pack",
    )(*(in_hbm(array) for array in (q, k, v, g, norm, delta)))


def nt(a, b):
    return lax.dot_general(a, b, (((1,), (1,)), ((), ())), preferred_element_type=jnp.float32)


def nn(a, b):
    return jnp.dot(a, b, preferred_element_type=jnp.float32)


def message_of(member):
    low = lax.axis_index("low")
    first, second = (order.index(member) for order in ORDERS)
    place = jnp.where(low // 2 % 2 == 0, first, second)
    return jnp.bitwise_xor(place, (TEAM - 1) * (low % 2))


def attend_kernel(swap_ref, docs_ref, in_ref, out_ref):
    span = SPOTS * TOK
    per_member = out_ref.shape[2] // HEAD
    swapped = swap_ref[0] != 0
    places = [message_of(member) for member in range(TEAM)]

    def unit(side, head):
        lanes = slice(head * HEAD, (head + 1) * HEAD)
        own = places[side * SPOTS : (side + 1) * SPOTS]
        other = places[(1 - side) * SPOTS : (2 - side) * SPOTS]
        target = [jnp.where(swapped, theirs, ours) for ours, theirs in zip(own, other)]

        def whole(slot):
            rows = slice((head * 4 + slot) * TOK, (head * 4 + slot + 1) * TOK)
            return jnp.concatenate([in_ref[place, rows, :] for place in own], axis=0)

        q, k, v, g = (whole(slot) for slot in range(4))
        k_turned = k.T
        dk = jnp.zeros((span, HEAD), jnp.float32)
        dv = jnp.zeros((span, HEAD), jnp.float32)
        for first in range(0, SPOTS, QUERY_SPOTS):
            spots = range(first, first + QUERY_SPOTS)
            columns = slice(first * TOK, (first + QUERY_SPOTS) * TOK)
            stats = [
                in_ref[own[spot], per_member * 4 * TOK :, :].astype(jnp.float32)
                for spot in spots
            ]
            norms = [stat[2 * head : 2 * head + 1] for stat in stats]
            delta = jnp.concatenate([stat[2 * head + 1 : 2 * head + 2] for stat in stats], axis=1)
            scores = nt(k, q[columns])
            dprobs = nt(v, g[columns])
            probs_low, dscores = [], []
            for key_spot in range(SPOTS):
                rows = slice(key_spot * TOK, (key_spot + 1) * TOK)
                key_doc = docs_ref[side, key_spot]
                bias = jnp.concatenate(
                    [
                        jnp.where(docs_ref[side, spot] == key_doc, norm * -LOG2E, MASKED)
                        for spot, norm in zip(spots, norms)
                    ],
                    axis=1,
                )
                probs = jnp.exp2(scores[rows] * (ROOT * LOG2E) + bias)
                probs_low.append(probs.astype(jnp.bfloat16))
                dscores.append((probs * (dprobs[rows] - delta)).astype(jnp.bfloat16))
            probs_low = jnp.concatenate(probs_low, axis=0)
            dscores = jnp.concatenate(dscores, axis=0)
            dk = dk + nn(dscores, q[columns])
            dv = dv + nn(probs_low, g[columns])
            dq = (nn(k_turned, dscores) * ROOT).T.astype(jnp.bfloat16)
            for place, spot in enumerate(spots):
                out_ref[target[spot], :TOK, lanes] = dq[place * TOK : (place + 1) * TOK]
        dk = (dk * ROOT).astype(jnp.bfloat16)
        dv = dv.astype(jnp.bfloat16)
        for spot in range(SPOTS):
            rows = slice(spot * TOK, (spot + 1) * TOK)
            out_ref[target[spot], TOK : 2 * TOK, lanes] = dk[rows]
            out_ref[target[spot], 2 * TOK :, lanes] = dv[rows]

    for side in range(SIDES):
        for head in range(per_member):
            unit(side, head)


def attend(swap, docs, messages):
    span = SPOTS * TOK
    per_member = messages.shape[1] // (4 * TOK)
    units = SIDES * per_member
    scalars = pl.BlockSpec(memory_space=pltpu.SMEM)
    return pl.pallas_call(
        attend_kernel,
        out_shape=pltpu.VMEM((TEAM, OUT_ROWS, per_member * HEAD), jnp.bfloat16),
        in_specs=[scalars, scalars, LOCAL],
        out_specs=LOCAL,
        compiler_params=PARAMS,
        cost_estimate=pl.CostEstimate(
            flops=units * 10 * span * span * HEAD,
            bytes_accessed=4 << 20,
            transcendentals=units * span * span,
        ),
        name="attend",
    )(swap, docs, in_vmem(messages))


def unpack_kernel(in_ref, q_ref, k_ref, v_ref, sems):
    width = in_ref.shape[2]
    copies = start_all(
        [
            pltpu.make_async_copy(
                in_ref.at[member, pl.ds(slot * TOK, TOK), :],
                ref.at[0, :, pl.ds(member * width, width)],
                sems.at[member, slot],
            )
            for member in range(TEAM)
            for slot, ref in enumerate((q_ref, k_ref, v_ref))
        ]
    )
    for copy in copies:
        copy.wait()


def unpack(messages):
    shape = (1, TOK, TEAM * messages.shape[2])
    return pl.pallas_call(
        unpack_kernel,
        out_shape=(pltpu.HBM(shape, jnp.bfloat16),) * 3,
        in_specs=[LOCAL],
        out_specs=(ANYWHERE,) * 3,
        scratch_shapes=[pltpu.SemaphoreType.DMA((TEAM, 3))],
        compiler_params=PARAMS,
        name="unpack",
    )(in_vmem(messages))


def exchange(messages):
    axes = ("side", "low", "bin", "spot")
    _, lows, bins, _ = (lax.axis_size(axis) for axis in axes)
    teams = [
        [
            ((member // SPOTS * lows + low) * bins + place) * SPOTS + member % SPOTS
            for member in ORDERS[low // 2 % 2][:: -1 if low % 2 else 1]
        ]
        for low in range(lows)
        for place in range(bins)
    ]
    return lax.all_to_all(messages, axes, 0, 0, tiled=True, axis_index_groups=teams)


def body(q, k, v, g, norm, delta, doc_lengths, bin_dest):
    groups = lax.axis_size("low")
    low = lax.axis_index("low")
    bin_index = lax.axis_index("bin")
    swap = (bin_dest[low, bin_index] != low).astype(jnp.int32)[None]
    lengths = doc_lengths.reshape((SIDES, groups) + doc_lengths.shape[1:])[:, low, bin_index]
    ends = jnp.cumsum(lengths, axis=1)
    docs = jnp.sum(
        (ends[:, None, :] <= jnp.arange(SPOTS, dtype=jnp.int32)[None, :, None]).astype(jnp.int32),
        axis=2,
    )
    packed = pack(q, k, v, g, jnp.transpose(norm[0]), jnp.transpose(delta[0]))
    return unpack(exchange(attend(swap, docs, exchange(packed))))


def solution(mesh):
    dp, ctx = mesh.devices.shape
    fine = Mesh(
        mesh.devices.reshape(SIDES, dp // SIDES, ctx // SPOTS, SPOTS),
        ("side", "low", "bin", "spot"),
    )
    split = P(("side", "low"), ("bin", "spot"), None)
    return jax.shard_map(
        body,
        mesh=fine,
        in_specs=(split,) * 6 + (P(), P()),
        out_specs=(split,) * 3,
        check_vma=False,
    )
```

```python
import math

import jax
import jax.numpy as jnp
from jax import lax
from jax.experimental import pallas as pl
from jax.experimental.pallas import tpu as pltpu
from jax.sharding import Mesh
from jax.sharding import PartitionSpec as P

TOK = 128
HEAD = 128
SIDES = 2
SPOTS = 4
TEAM = SIDES * SPOTS
ORDERS = ((0, 2, 1, 3, 5, 7, 4, 6), (0, 4, 2, 6, 3, 7, 1, 5))
STAT_ROWS = 16
OUT_ROWS = 3 * TOK
MASKED = -1e30
ROOT = 1.0 / math.sqrt(HEAD)
LOG2E = math.log2(math.e)
VMEM_LIMIT = 24 << 20


def start_all(copies):
    for copy in copies:
        copy.start()
    return copies


def pack_kernel(q_ref, k_ref, v_ref, g_ref, norm_ref, delta_ref, out_ref, held, stats, sems, stat_sems):
    per_member = held.shape[2] // (TEAM * HEAD)
    stat_copies = start_all(
        [
            pltpu.make_async_copy(ref, stats.at[slot], stat_sems.at[slot])
            for slot, ref in enumerate((norm_ref, delta_ref))
        ]
    )
    copies = start_all(
        [
            pltpu.make_async_copy(ref.at[0], held.at[slot], sems.at[slot])
            for slot, ref in enumerate((q_ref, k_ref, v_ref, g_ref))
        ]
    )
    for copy in stat_copies:
        copy.wait()
    norm = stats[0].astype(jnp.float32)
    delta = stats[1].astype(jnp.float32)
    row = lax.broadcasted_iota(jnp.int32, (STAT_ROWS, HEAD), 0)
    for member in range(TEAM):
        tile = jnp.zeros((STAT_ROWS, HEAD), jnp.float32)
        for place in range(per_member):
            head = member * per_member + place
            tile = jnp.where(row == 2 * place, norm[head : head + 1], tile)
            tile = jnp.where(row == 2 * place + 1, delta[head : head + 1], tile)
        out_ref[member, per_member * 4 * TOK :, :] = tile.astype(jnp.bfloat16)
    for slot, copy in enumerate(copies):
        copy.wait()
        for head in range(TEAM * per_member):
            member, place = divmod(head, per_member)
            first = (place * 4 + slot) * TOK
            out_ref[member, first : first + TOK, :] = held[
                slot, :, head * HEAD : (head + 1) * HEAD
            ]


def in_hbm(array):
    return pltpu.with_memory_space_constraint(array, pltpu.HBM)


def in_vmem(array):
    return pltpu.with_memory_space_constraint(array, pltpu.VMEM)


ANYWHERE = pl.BlockSpec(memory_space=pl.ANY)
LOCAL = pl.BlockSpec(memory_space=pltpu.VMEM)
PARAMS = pltpu.CompilerParams(vmem_limit_bytes=VMEM_LIMIT)


def pack(q, k, v, g, norm, delta):
    rows = q.shape[2] // (TEAM * HEAD) * 4 * TOK + STAT_ROWS
    return pl.pallas_call(
        pack_kernel,
        out_shape=pltpu.VMEM((TEAM, rows, HEAD), jnp.bfloat16),
        in_specs=[ANYWHERE] * 6,
        out_specs=LOCAL,
        scratch_shapes=[
            pltpu.VMEM((4,) + q.shape[1:], jnp.bfloat16),
            pltpu.VMEM((2,) + norm.shape, jnp.bfloat16),
            pltpu.SemaphoreType.DMA((4,)),
            pltpu.SemaphoreType.DMA((2,)),
        ],
        compiler_params=PARAMS,
        name="pack",
    )(*(in_hbm(array) for array in (q, k, v, g, norm, delta)))


def nt(a, b):
    return lax.dot_general(a, b, (((1,), (1,)), ((), ())), preferred_element_type=jnp.float32)


def nn(a, b):
    return jnp.dot(a, b, preferred_element_type=jnp.float32)


def message_of(member):
    low = lax.axis_index("low")
    first, second = (order.index(member) for order in ORDERS)
    place = jnp.where(low // 2 % 2 == 0, first, second)
    return jnp.bitwise_xor(place, (TEAM - 1) * (low % 2))


def attend_kernel(swap_ref, docs_ref, in_ref, out_ref):
    span = SPOTS * TOK
    per_member = out_ref.shape[2] // HEAD
    swapped = swap_ref[0] != 0
    places = [message_of(member) for member in range(TEAM)]

    def whole(side, head, slot):
        rows = slice((head * 4 + slot) * TOK, (head * 4 + slot + 1) * TOK)
        own = places[side * SPOTS : (side + 1) * SPOTS]
        return jnp.concatenate([in_ref[place, rows, :] for place in own], axis=0)

    def multiply(side, head):
        q, k, v, g = (whole(side, head, slot) for slot in range(4))
        return nt(k, q), nt(v, g)

    def weigh(side, head, scores, dprobs):
        own = places[side * SPOTS : (side + 1) * SPOTS]
        stats = [in_ref[place, per_member * 4 * TOK :, :].astype(jnp.float32) for place in own]
        norms = [stat[2 * head : 2 * head + 1] * -LOG2E for stat in stats]
        delta = jnp.concatenate([stat[2 * head + 1 : 2 * head + 2] for stat in stats], axis=1)
        probs_low, dscores = [], []
        for key_spot in range(SPOTS):
            rows = slice(key_spot * TOK, (key_spot + 1) * TOK)
            key_doc = docs_ref[side, key_spot]
            bias = jnp.concatenate(
                [
                    jnp.where(docs_ref[side, spot] == key_doc, norm, MASKED)
                    for spot, norm in enumerate(norms)
                ],
                axis=1,
            )
            probs = jnp.exp2(scores[rows] * (ROOT * LOG2E) + bias)
            probs_low.append(probs.astype(jnp.bfloat16))
            dscores.append((probs * (dprobs[rows] - delta)).astype(jnp.bfloat16))
        return jnp.concatenate(probs_low, axis=0), jnp.concatenate(dscores, axis=0)

    def finish(side, head, probs_low, dscores):
        lanes = slice(head * HEAD, (head + 1) * HEAD)
        own = places[side * SPOTS : (side + 1) * SPOTS]
        other = places[(1 - side) * SPOTS : (2 - side) * SPOTS]
        q, k, _, g = (whole(side, head, slot) for slot in range(4))
        dq = (nn(k.T, dscores) * ROOT).T.astype(jnp.bfloat16)
        dk = (nn(dscores, q) * ROOT).astype(jnp.bfloat16)
        dv = nn(probs_low, g).astype(jnp.bfloat16)
        for spot in range(SPOTS):
            target = jnp.where(swapped, other[spot], own[spot])
            rows = slice(spot * TOK, (spot + 1) * TOK)
            for slot, grad in enumerate((dq, dk, dv)):
                out_ref[target, slot * TOK : (slot + 1) * TOK, lanes] = grad[rows]

    units = [(side, head) for side in range(SIDES) for head in range(per_member)]
    ahead = multiply(*units[0])
    for number, unit in enumerate(units):
        products = ahead
        if number + 1 < len(units):
            ahead = multiply(*units[number + 1])
        finish(*unit, *weigh(*unit, *products))


def attend(swap, docs, messages):
    span = SPOTS * TOK
    per_member = messages.shape[1] // (4 * TOK)
    units = SIDES * per_member
    scalars = pl.BlockSpec(memory_space=pltpu.SMEM)
    return pl.pallas_call(
        attend_kernel,
        out_shape=pltpu.VMEM((TEAM, OUT_ROWS, per_member * HEAD), jnp.bfloat16),
        in_specs=[scalars, scalars, LOCAL],
        out_specs=LOCAL,
        compiler_params=PARAMS,
        cost_estimate=pl.CostEstimate(
            flops=units * 10 * span * span * HEAD,
            bytes_accessed=4 << 20,
            transcendentals=units * span * span,
        ),
        name="attend",
    )(swap, docs, in_vmem(messages))


def unpack_kernel(in_ref, q_ref, k_ref, v_ref, sems):
    width = in_ref.shape[2]
    copies = start_all(
        [
            pltpu.make_async_copy(
                in_ref.at[member, pl.ds(slot * TOK, TOK), :],
                ref.at[0, :, pl.ds(member * width, width)],
                sems.at[member, slot],
            )
            for member in range(TEAM)
            for slot, ref in enumerate((q_ref, k_ref, v_ref))
        ]
    )
    for copy in copies:
        copy.wait()


def unpack(messages):
    shape = (1, TOK, TEAM * messages.shape[2])
    return pl.pallas_call(
        unpack_kernel,
        out_shape=(pltpu.HBM(shape, jnp.bfloat16),) * 3,
        in_specs=[LOCAL],
        out_specs=(ANYWHERE,) * 3,
        scratch_shapes=[pltpu.SemaphoreType.DMA((TEAM, 3))],
        compiler_params=PARAMS,
        name="unpack",
    )(in_vmem(messages))


def exchange(messages):
    axes = ("side", "low", "bin", "spot")
    _, lows, bins, _ = (lax.axis_size(axis) for axis in axes)
    teams = [
        [
            ((member // SPOTS * lows + low) * bins + place) * SPOTS + member % SPOTS
            for member in ORDERS[low // 2 % 2][:: -1 if low % 2 else 1]
        ]
        for low in range(lows)
        for place in range(bins)
    ]
    return lax.all_to_all(messages, axes, 0, 0, tiled=True, axis_index_groups=teams)


def body(q, k, v, g, norm, delta, doc_lengths, bin_dest):
    groups = lax.axis_size("low")
    low = lax.axis_index("low")
    bin_index = lax.axis_index("bin")
    swap = (bin_dest[low, bin_index] != low).astype(jnp.int32)[None]
    lengths = doc_lengths.reshape((SIDES, groups) + doc_lengths.shape[1:])[:, low, bin_index]
    ends = jnp.cumsum(lengths, axis=1)
    docs = jnp.sum(
        (ends[:, None, :] <= jnp.arange(SPOTS, dtype=jnp.int32)[None, :, None]).astype(jnp.int32),
        axis=2,
    )
    packed = pack(q, k, v, g, jnp.transpose(norm[0]), jnp.transpose(delta[0]))
    return unpack(exchange(attend(swap, docs, exchange(packed))))


def solution(mesh):
    dp, ctx = mesh.devices.shape
    fine = Mesh(
        mesh.devices.reshape(SIDES, dp // SIDES, ctx // SPOTS, SPOTS),
        ("side", "low", "bin", "spot"),
    )
    split = P(("side", "low"), ("bin", "spot"), None)
    return jax.shard_map(
        body,
        mesh=fine,
        in_specs=(split,) * 6 + (P(), P()),
        out_specs=(split,) * 3,
        check_vma=False,
    )
```

```python
import math

import jax
import jax.numpy as jnp
from jax import lax
from jax.experimental import pallas as pl
from jax.experimental.pallas import tpu as pltpu
from jax.sharding import Mesh
from jax.sharding import PartitionSpec as P

TOK = 128
HEAD = 128
SIDES = 2
SPOTS = 4
TEAM = SIDES * SPOTS
ORDERS = ((0, 2, 1, 3, 5, 7, 4, 6), (0, 4, 2, 6, 3, 7, 1, 5))
STAT_ROWS = 16
OUT_ROWS = 3 * TOK
MASKED = -1e30
ROOT = 1.0 / math.sqrt(HEAD)
LOG2E = math.log2(math.e)
VMEM_LIMIT = 24 << 20


def start_all(copies):
    for copy in copies:
        copy.start()
    return copies


def pack_kernel(q_ref, k_ref, v_ref, g_ref, norm_ref, delta_ref, out_ref, held, stats, sems, stat_sems):
    per_member = held.shape[2] // (TEAM * HEAD)
    stat_copies = start_all(
        [
            pltpu.make_async_copy(ref, stats.at[slot], stat_sems.at[slot])
            for slot, ref in enumerate((norm_ref, delta_ref))
        ]
    )
    copies = start_all(
        [
            pltpu.make_async_copy(ref.at[0], held.at[slot], sems.at[slot])
            for slot, ref in enumerate((q_ref, k_ref, v_ref, g_ref))
        ]
    )
    for copy in stat_copies:
        copy.wait()
    norm = stats[0].astype(jnp.float32)
    delta = stats[1].astype(jnp.float32)
    row = lax.broadcasted_iota(jnp.int32, (STAT_ROWS, HEAD), 0)
    for member in range(TEAM):
        tile = jnp.zeros((STAT_ROWS, HEAD), jnp.float32)
        for place in range(per_member):
            head = member * per_member + place
            tile = jnp.where(row == 2 * place, norm[head : head + 1], tile)
            tile = jnp.where(row == 2 * place + 1, delta[head : head + 1], tile)
        out_ref[member, per_member * 4 * TOK :, :] = tile.astype(jnp.bfloat16)
    for slot, copy in enumerate(copies):
        copy.wait()
        for head in range(TEAM * per_member):
            member, place = divmod(head, per_member)
            first = (place * 4 + slot) * TOK
            out_ref[member, first : first + TOK, :] = held[
                slot, :, head * HEAD : (head + 1) * HEAD
            ]


def in_hbm(array):
    return pltpu.with_memory_space_constraint(array, pltpu.HBM)


def in_vmem(array):
    return pltpu.with_memory_space_constraint(array, pltpu.VMEM)


ANYWHERE = pl.BlockSpec(memory_space=pl.ANY)
LOCAL = pl.BlockSpec(memory_space=pltpu.VMEM)
PARAMS = pltpu.CompilerParams(vmem_limit_bytes=VMEM_LIMIT)


def pack(q, k, v, g, norm, delta):
    rows = q.shape[2] // (TEAM * HEAD) * 4 * TOK + STAT_ROWS
    return pl.pallas_call(
        pack_kernel,
        out_shape=pltpu.VMEM((TEAM, rows, HEAD), jnp.bfloat16),
        in_specs=[ANYWHERE] * 6,
        out_specs=LOCAL,
        scratch_shapes=[
            pltpu.VMEM((4,) + q.shape[1:], jnp.bfloat16),
            pltpu.VMEM((2,) + norm.shape, jnp.bfloat16),
            pltpu.SemaphoreType.DMA((4,)),
            pltpu.SemaphoreType.DMA((2,)),
        ],
        compiler_params=PARAMS,
        name="pack",
    )(*(in_hbm(array) for array in (q, k, v, g, norm, delta)))


def nt(a, b):
    return lax.dot_general(a, b, (((1,), (1,)), ((), ())), preferred_element_type=jnp.float32)


def nn(a, b):
    return jnp.dot(a, b, preferred_element_type=jnp.float32)


def message_of(member):
    low = lax.axis_index("low")
    first, second = (order.index(member) for order in ORDERS)
    place = jnp.where(low // 2 % 2 == 0, first, second)
    return jnp.bitwise_xor(place, (TEAM - 1) * (low % 2))


def attend_kernel(swap_ref, docs_ref, in_ref, out_ref):
    span = SPOTS * TOK
    per_member = out_ref.shape[2] // HEAD
    swapped = swap_ref[0] != 0
    places = [message_of(member) for member in range(TEAM)]

    def whole(side, head, slot):
        rows = slice((head * 4 + slot) * TOK, (head * 4 + slot + 1) * TOK)
        own = places[side * SPOTS : (side + 1) * SPOTS]
        return jnp.concatenate([in_ref[place, rows, :] for place in own], axis=0)

    def multiply(side, head):
        q, k, v, g = (whole(side, head, slot) for slot in range(4))
        return nt(k, q), nt(v, g)

    def weigh(side, head, scores, dprobs):
        own = places[side * SPOTS : (side + 1) * SPOTS]
        stats = [in_ref[place, per_member * 4 * TOK :, :].astype(jnp.float32) for place in own]
        norms = [stat[2 * head : 2 * head + 1] * -LOG2E for stat in stats]
        delta = jnp.concatenate([stat[2 * head + 1 : 2 * head + 2] for stat in stats], axis=1)
        probs_low, dscores = [], []
        for key_spot in range(SPOTS):
            rows = slice(key_spot * TOK, (key_spot + 1) * TOK)
            key_doc = docs_ref[side, key_spot]
            bias = jnp.concatenate(
                [
                    jnp.where(docs_ref[side, spot] == key_doc, norm, MASKED)
                    for spot, norm in enumerate(norms)
                ],
                axis=1,
            )
            probs = jnp.exp2(scores[rows] * (ROOT * LOG2E) + bias)
            probs_low.append(probs.astype(jnp.bfloat16))
            dscores.append((probs * (dprobs[rows] - delta)).astype(jnp.bfloat16))
        return jnp.concatenate(probs_low, axis=0), jnp.concatenate(dscores, axis=0)

    def finish(side, head, probs_low, dscores):
        lanes = slice(head * HEAD, (head + 1) * HEAD)
        own = places[side * SPOTS : (side + 1) * SPOTS]
        other = places[(1 - side) * SPOTS : (2 - side) * SPOTS]
        q, k, _, g = (whole(side, head, slot) for slot in range(4))
        dq = (nn(k.T, dscores) * ROOT).T.astype(jnp.bfloat16)
        dk = (nn(dscores, q) * ROOT).astype(jnp.bfloat16)
        dv = nn(probs_low, g).astype(jnp.bfloat16)
        for spot in range(SPOTS):
            target = jnp.where(swapped, other[spot], own[spot])
            rows = slice(spot * TOK, (spot + 1) * TOK)
            for slot, grad in enumerate((dq, dk, dv)):
                out_ref[target, slot * TOK : (slot + 1) * TOK, lanes] = grad[rows]

    units = [(side, head) for side in range(SIDES) for head in range(per_member)]
    ahead, weights = multiply(*units[0]), None
    for number, unit in enumerate(units):
        products = ahead
        if number + 1 < len(units):
            ahead = multiply(*units[number + 1])
        if weights is not None:
            finish(*units[number - 1], *weights)
        weights = weigh(*unit, *products)
    finish(*units[-1], *weights)


def attend(swap, docs, messages):
    span = SPOTS * TOK
    per_member = messages.shape[1] // (4 * TOK)
    units = SIDES * per_member
    scalars = pl.BlockSpec(memory_space=pltpu.SMEM)
    return pl.pallas_call(
        attend_kernel,
        out_shape=pltpu.VMEM((TEAM, OUT_ROWS, per_member * HEAD), jnp.bfloat16),
        in_specs=[scalars, scalars, LOCAL],
        out_specs=LOCAL,
        compiler_params=PARAMS,
        cost_estimate=pl.CostEstimate(
            flops=units * 10 * span * span * HEAD,
            bytes_accessed=4 << 20,
            transcendentals=units * span * span,
        ),
        name="attend",
    )(swap, docs, in_vmem(messages))


def unpack_kernel(in_ref, q_ref, k_ref, v_ref, sems):
    width = in_ref.shape[2]
    copies = start_all(
        [
            pltpu.make_async_copy(
                in_ref.at[member, pl.ds(slot * TOK, TOK), :],
                ref.at[0, :, pl.ds(member * width, width)],
                sems.at[member, slot],
            )
            for member in range(TEAM)
            for slot, ref in enumerate((q_ref, k_ref, v_ref))
        ]
    )
    for copy in copies:
        copy.wait()


def unpack(messages):
    shape = (1, TOK, TEAM * messages.shape[2])
    return pl.pallas_call(
        unpack_kernel,
        out_shape=(pltpu.HBM(shape, jnp.bfloat16),) * 3,
        in_specs=[LOCAL],
        out_specs=(ANYWHERE,) * 3,
        scratch_shapes=[pltpu.SemaphoreType.DMA((TEAM, 3))],
        compiler_params=PARAMS,
        name="unpack",
    )(in_vmem(messages))


def exchange(messages):
    axes = ("side", "low", "bin", "spot")
    _, lows, bins, _ = (lax.axis_size(axis) for axis in axes)
    teams = [
        [
            ((member // SPOTS * lows + low) * bins + place) * SPOTS + member % SPOTS
            for member in ORDERS[low // 2 % 2][:: -1 if low % 2 else 1]
        ]
        for low in range(lows)
        for place in range(bins)
    ]
    return lax.all_to_all(messages, axes, 0, 0, tiled=True, axis_index_groups=teams)


def body(q, k, v, g, norm, delta, doc_lengths, bin_dest):
    groups = lax.axis_size("low")
    low = lax.axis_index("low")
    bin_index = lax.axis_index("bin")
    swap = (bin_dest[low, bin_index] != low).astype(jnp.int32)[None]
    lengths = doc_lengths.reshape((SIDES, groups) + doc_lengths.shape[1:])[:, low, bin_index]
    ends = jnp.cumsum(lengths, axis=1)
    docs = jnp.sum(
        (ends[:, None, :] <= jnp.arange(SPOTS, dtype=jnp.int32)[None, :, None]).astype(jnp.int32),
        axis=2,
    )
    packed = pack(q, k, v, g, jnp.transpose(norm[0]), jnp.transpose(delta[0]))
    return unpack(exchange(attend(swap, docs, exchange(packed))))


def solution(mesh):
    dp, ctx = mesh.devices.shape
    fine = Mesh(
        mesh.devices.reshape(SIDES, dp // SIDES, ctx // SPOTS, SPOTS),
        ("side", "low", "bin", "spot"),
    )
    split = P(("side", "low"), ("bin", "spot"), None)
    return jax.shard_map(
        body,
        mesh=fine,
        in_specs=(split,) * 6 + (P(), P()),
        out_specs=(split,) * 3,
        check_vma=False,
    )
```
